32 devices in a mesh: rep: 8 (over z, x), shard: 4 (over y, core).
Axes of the slice: x: 2, y: 2, z: 4, core: 2. Of those that a mesh axis runs over, the one named last changes fastest.
Arguments:
- attn: bfloat16 [8, 1536, 2560], P('rep', 'shard'), may hold values from -6 to 6
- resid: bfloat16 [8, 1536, 2560], P('rep', 'shard'), may hold values from -200 to 200
- cotangent: bfloat16 [8, 1536, 2560], P('rep', 'shard'), may hold values from -6 to 6
- gain: float32 [2560], replicated, may hold values from 0.1 to 1.9
- numer: float32 [8, 2560, 2560], P('rep', 'shard'), may hold values from -6 to 6
- pweight: float32 [8], P('rep'), may hold values from 0.5 to 2
- round_bit: int32 [1], replicated, may hold values from 0 to 2
Outputs:
- new_numer: float32 [8, 2560, 2560], P('rep', 'shard')
- new_pweight: float32 [8], P('rep')
The draws below stay inside these ranges and needn't reach their ends.
All inputs are finite; a program needn't handle non-finite values.
Results may differ from the reference program's by a relative error of at most 0.008.
Values may be sent and summed in bfloat16 or wider, within the bound.
A program may use at most 192 MiB of HBM per device.

```python
import math
import jax
import jax.numpy as jnp
from jax import lax

DIN = 2560
DOUT = 2560
TOK_DEV = 384
TOKENS = 1536
BITS = 3
N_REP = 8
N_SHARD = 4


def raised(drawn, own_key, source, target, parts, factor):
    def block_of(dim):
        return (jnp.arange(drawn.shape[dim]) // (drawn.shape[dim] // parts)).reshape((-1,) + (1,) * (drawn.ndim - 1 - dim))

    one_side = jax.random.permutation(own_key, parts)[block_of(target)]
    far = (block_of(target) + parts // 2) % parts
    return jnp.where((block_of(source) == one_side) | (block_of(source) == far), factor * drawn, drawn)


def level_of(key, shape, shards, smallest, top_value):
    def one(position, blocks):
        draws = jax.random.uniform(jax.random.fold_in(jax.random.fold_in(key, 6), position), (blocks,), jnp.float32, smallest / len(shards), top_value / len(shards))
        return jnp.repeat(jnp.exp(draws), shape[position] // blocks).reshape((-1,) + (1,) * (len(shape) - position - 1))

    factor_of = one(*shards[0])
    for cut in shards[1:]:
        factor_of = factor_of * one(*cut)
    return factor_of


def bell_draw(key, dims, spread, bound, split=(), kind=jnp.bfloat16):
    level = level_of(key, dims, split, -0.22, 0.18) if split else 1.0
    values = jax.random.normal(key, dims, jnp.float32) * spread * level
    return jnp.minimum(jnp.maximum(values, -bound), bound).astype(kind)


def heavy_noise(own_key, shape, deviation, reach, shards, heavy, held_as=jnp.bfloat16):
    result = deviation * jax.random.normal(own_key, shape, jnp.float32)
    if shards:
        result = result * level_of(own_key, shape, shards, -0.22, 0.18)
    return jnp.clip(raised(result, jax.random.fold_in(own_key, 3), *heavy), -reach, reach).astype(held_as)


def setup_inputs(seed: int = 0) -> dict:
    streams_of = jax.random.split(jax.random.key(seed), 8)
    return {
        "attn": heavy_noise(streams_of[0], (N_REP, TOKENS, DIN), 1.0, 6.0, ((0, 8), (1, 4)), (1, 2, 4, 2.0)),
        "resid": bell_draw(streams_of[1], (N_REP, TOKENS, DOUT), 40.0, 200.0, ((0, 8), (1, 4))),
        "cotangent": bell_draw(streams_of[2], (N_REP, TOKENS, DOUT), 1.0, 6.0, ((0, 8), (1, 4))),
        "gain": jnp.clip(1.0 + 0.18 * jax.random.normal(streams_of[3], (DOUT,), jnp.float32), 0.1, 1.9),
        "numer": bell_draw(streams_of[4], (N_REP, DIN, DOUT), 1.0, 6.0, ((0, 8), (1, 4)), jnp.float32),
        "pweight": jnp.clip(jnp.exp(math.log(2.0) - 1.3862944 * jax.random.uniform(streams_of[5], (N_REP,), jnp.float32) ** level_of(streams_of[5], (N_REP,), ((0, 8),), -0.2, 0.2)), 0.5, 2.0),
        "round_bit": jax.random.randint(streams_of[6], (1,), 0, BITS).astype(jnp.int32),
    }


EPS = 1e-05
learning_rate = 0.5

def replica_step(item):
    attn_r, resid_r, cot_r, numer_r, weight_r, gain = item
    weights = (numer_r / weight_r).astype(jnp.bfloat16)
    pre = resid_r.astype(jnp.float32) + jnp.dot(attn_r, weights, preferred_element_type=jnp.float32)
    inv = lax.rsqrt(lax.optimization_barrier(jnp.mean(pre * pre, axis=1, keepdims=True)) + EPS)
    normed = pre * inv
    dnorm = cot_r.astype(jnp.float32) * gain
    dpre = (inv * (dnorm - normed * lax.optimization_barrier(jnp.mean(dnorm * normed, axis=1, keepdims=True)))).astype(jnp.bfloat16)
    groups_a = attn_r.reshape(N_SHARD, TOK_DEV, DIN)
    groups_d = dpre.reshape(N_SHARD, TOK_DEV, DOUT)

    def add_group(total, pair):
        part = jnp.dot(pair[0].T, pair[1], preferred_element_type=jnp.float32)
        return (total + part.astype(jnp.bfloat16).astype(jnp.float32), None)
    grad, _ = lax.scan(add_group, jnp.zeros((DIN, DOUT), jnp.float32), (groups_a, groups_d))
    return numer_r - learning_rate * grad

def reference(attn, resid, cotangent, gain, numer, pweight, round_bit):
    gains = jnp.broadcast_to(gain, (N_REP, DOUT))
    stepped = lax.map(replica_step, (attn, resid, cotangent, numer, pweight, gains))
    partner = jnp.bitwise_xor(jnp.arange(N_REP, dtype=jnp.int32), jnp.left_shift(jnp.int32(1), round_bit[0].astype(jnp.int32)))
    new_numer = 0.5 * (stepped + stepped[partner])
    new_pweight = 0.5 * (pweight + pweight[partner])
    return (new_numer, new_pweight)
```

```python
import functools

import jax
import jax.numpy as jnp
from jax import lax
from jax.experimental import pallas as pl
from jax.experimental.pallas import tpu as pltpu
from jax.sharding import PartitionSpec as P

EPS = 1e-05
learning_rate = 0.5


def shortened(shard):

    def short(part):
        return part.astype(jnp.bfloat16) if part.dtype == jnp.float32 else part

    return jax.tree.map(short, shard)


def from_partner(shard, axis, apart):
    return lax.ppermute(shard, axis, [(i, i ^ 1 << apart) for i in range(lax.axis_size(axis))])


def on_device(attn, resid, cotangent, gain, numer, pweight, round_bit):
    acts = attn[0]
    weight_rows = (numer[0] / pweight[0]).astype(jnp.bfloat16)
    columns = acts
    pre = resid[0].astype(jnp.float32) + jnp.dot(
        columns,
        lax.all_gather(weight_rows, "shard", axis=0, tiled=True),
        preferred_element_type=jnp.float32,
    )
    inv = lax.rsqrt(jnp.mean(pre * pre, axis=1, keepdims=True) + EPS)
    normed = pre * inv
    dnorm = cotangent[0].astype(jnp.float32) * gain
    dpre = (inv * (dnorm - normed * jnp.mean(dnorm * normed, axis=1, keepdims=True))).astype(
        jnp.bfloat16
    )
    columns = acts
    grad = lax.psum_scatter(
        lax.dot_general(
            columns, dpre, (((0,), (0,)), ((), ())), preferred_element_type=jnp.float32
        ).astype(jnp.bfloat16),
        "shard",
        scatter_dimension=0,
        tiled=True,
    ).astype(jnp.float32)
    stepped = numer[0] - learning_rate * grad
    levels = lax.axis_size("rep").bit_length() - 1

    def pushed(bit):

        def send_pair(pair):
            return jax.tree.map(
                lambda part, own: part.astype(own.dtype),
                from_partner(shortened(pair), "rep", bit),
                pair,
            )

        return send_pair

    other_numer, other_weight = lax.switch(
        round_bit[0], [pushed(level) for level in range(levels)], (stepped, pweight)
    )
    new_numer = (0.5 * (stepped + other_numer))[None]
    new_pweight = 0.5 * (pweight + other_weight)
    return (new_numer, new_pweight)


def fused_kernel(
    bit, chunk, block,
    attn, resid, cot, gain, numer, pw, out, out_pw,
    acts, acts_t, res, ct, gn, nm, wt, pre, p_send, p_recv, st_send, st_recv,
    inv, inv_m, dp, s_send, s_recv, pw_send, pw_recv,
    loc, out_loc, core_s, core_r, relay_s, relay_r, stat_s, stat_r, out_s, out_r,
    ya_s, ya_r, yp_s, yp_r, yd_s, yd_r, rep_s, rep_r, pws_s, pws_r,
):
    tokens, features = attn.shape
    rows = numer.shape[0]
    half = features // 2
    depth = 2 * rows
    chunks = tokens // chunk
    blocks = half // block
    shard = lax.axis_index("shard")
    rep = lax.axis_index("rep")
    core, chip = shard % 2, shard // 2
    apart = 1 << bit
    to_core = {"shard": chip * 2 + 1 - core}
    to_chip = {"shard": (1 - chip) * 2 + core}
    to_rep = {"rep": rep + apart - 2 * apart * ((rep // apart) % 2)}

    def remote(src, dst, send, recv, device):
        return pltpu.make_async_remote_copy(
            src_ref=src, dst_ref=dst, send_sem=send, recv_sem=recv,
            device_id=device, device_id_type=pl.DeviceIdType.MESH,
        )

    my_half = pl.ds(pl.multiple_of(core * half, half), half)
    its_half = pl.ds(pl.multiple_of((1 - core) * half, half), half)
    my_rows = pl.ds(pl.multiple_of(core * rows, rows), rows)
    its_rows = pl.ds(pl.multiple_of((1 - core) * rows, rows), rows)
    my_depth = pl.ds(pl.multiple_of(chip * depth, depth), depth)
    its_depth = pl.ds(pl.multiple_of((1 - chip) * depth, depth), depth)

    local = [
        pltpu.make_async_copy(numer.at[:, my_half], nm.at[my_rows], loc.at[0]),
        pltpu.make_async_copy(attn.at[:, my_depth], acts.at[0:tokens], loc.at[1]),
        pltpu.make_async_copy(resid.at[:, my_half], res.at[0:tokens], loc.at[2]),
        pltpu.make_async_copy(cot.at[:, my_half], ct.at[0:tokens], loc.at[3]),
        pltpu.make_async_copy(gain.at[:, my_half], gn, loc.at[4]),
    ]
    for copy in local:
        copy.start()

    barrier = pltpu.get_barrier_semaphore()
    for device in (to_core, to_chip, to_rep):
        pl.semaphore_signal(barrier, inc=1, device_id=device, device_id_type=pl.DeviceIdType.MESH)
    pl.semaphore_wait(barrier, 3)

    def part(slot, i):
        return pl.ds(slot * tokens + i * chunk, chunk)

    y_attn = [
        remote(attn.at[pl.ds(i * chunk, chunk), its_depth], acts.at[part(2, i)],
               ya_s.at[i], ya_r.at[i], to_chip)
        for i in range(chunks)
    ]
    for copy in y_attn:
        copy.start()
    to_other_core = [
        remote(numer.at[:, its_half], nm.at[my_rows], core_s.at[0], core_r.at[0], to_core),
        remote(attn.at[:, my_depth], acts.at[tokens:2 * tokens], core_s.at[1], core_r.at[1], to_core),
        remote(resid.at[:, its_half], res.at[tokens:2 * tokens], core_s.at[2], core_r.at[2], to_core),
        remote(cot.at[:, its_half], ct.at[tokens:2 * tokens], core_s.at[3], core_r.at[3], to_core),
    ]
    for copy in to_other_core:
        copy.start()
    weight = pw[0]
    pw_send[...] = jnp.full(pw_send.shape, weight, jnp.float32)
    pw_copy = remote(pw_send, pw_recv, pws_s, pws_r, to_rep)
    pw_copy.start()

    step = 32

    def divide(half_rows):
        def body(i, _):
            at = pl.ds(pl.multiple_of(half_rows + i * step, step), step)
            wt[at] = (nm[at] / weight).astype(jnp.bfloat16)
            return 0
        lax.fori_loop(0, rows // step, body, 0)

    local[0].wait()
    divide(core * rows)
    to_other_core[0].wait_recv()
    divide((1 - core) * rows)

    tile = min(256, half)

    def times_weights(at, store):
        def body(j, _):
            cols = pl.ds(pl.multiple_of(j * tile, tile), tile)
            store(cols, jnp.dot(acts[at], wt[:, cols], preferred_element_type=jnp.float32))
            return 0
        lax.fori_loop(0, half // tile, body, 0)

    relays, p_copies = [], {}

    def partial(slot, i):
        at = part(slot, i)

        def store(cols, value):
            p_send[at, cols] = value.astype(jnp.bfloat16)

        times_weights(part(slot + 2, i), store)
        n = 2 * i + slot
        copy = remote(p_send.at[at], p_recv.at[at], yp_s.at[n], yp_r.at[n], to_chip)
        copy.start()
        p_copies[n] = copy

    for i in range(chunks):
        y_attn[i].wait_recv()
        relay = remote(acts.at[part(2, i)], acts.at[part(3, i)], relay_s.at[i], relay_r.at[i], to_core)
        relay.start()
        relays.append(relay)
        partial(0, i)
        relay.wait_recv()
        partial(1, i)

    for copy in local[1:]:
        copy.wait()
    for copy in to_other_core[1:]:
        copy.wait_recv()

    def own(i, _):
        at = pl.ds(pl.multiple_of(i * chunk, chunk), chunk)

        def store(cols, value):
            pre[at, cols] = res[at, cols].astype(jnp.float32) + value

        times_weights(at, store)
        return 0

    lax.fori_loop(0, 2 * chunks, own, 0)

    def turn(i, _):
        at = pl.ds(pl.multiple_of(i * 128, 128), 128)
        acts_t[:, at] = acts[at].T
        return 0

    lax.fori_loop(0, 4 * tokens // 128, turn, 0)

    stats = {}
    for i in range(chunks):
        for slot in range(2):
            n = 2 * i + slot
            p_copies[n].wait_recv()

            def add(k, _):
                at = pl.ds(pl.multiple_of(slot * tokens + i * chunk + k * step, step), step)
                value = pre[at] + p_recv[at].astype(jnp.float32)
                pre[at] = value
                dnorm = ct[at].astype(jnp.float32) * gn[...]
                to = pl.ds(pl.multiple_of(k * step, step), step)
                st_send[n, 0, to] = jnp.broadcast_to(
                    jnp.sum(value * value, axis=1, keepdims=True), (step, 128))
                st_send[n, 1, to] = jnp.broadcast_to(
                    jnp.sum(value * dnorm, axis=1, keepdims=True), (step, 128))
                return 0

            lax.fori_loop(0, chunk // step, add, 0)
            m = 2 * i + 1 - slot
            copy = remote(st_send.at[n], st_recv.at[m], stat_s.at[n], stat_r.at[m], to_core)
            copy.start()
            stats[n] = copy

    for i in range(chunks):
        for slot in range(2):
            n = 2 * i + slot
            m = 2 * i + 1 - slot
            stats[m].wait_recv()
            at = part(slot, i)
            scale = lax.rsqrt((st_send[n, 0] + st_recv[n, 0]) * (1.0 / features) + EPS)
            inv[at] = scale
            inv_m[at] = scale * scale * ((st_send[n, 1] + st_recv[n, 1]) * (1.0 / features))

    d_copies = []
    for b in range(blocks):
        cols = slice(b * block, (b + 1) * block)

        def back(k, _):
            at = pl.ds(pl.multiple_of(k * step, step), step)
            dnorm = ct[at, cols].astype(jnp.float32) * gn[:, cols]
            scale = inv[at, 0:1]
            value = scale * (dnorm - pre[at, cols] * inv_m[at, 0:1])
            dp[b, at] = value.astype(jnp.bfloat16)
            return 0

        lax.fori_loop(0, 2 * tokens // step, back, 0)
        copy = remote(dp.at[b, 0:2 * tokens], dp.at[b, 2 * tokens:4 * tokens],
                      yd_s.at[b], yd_r.at[b], to_chip)
        copy.start()
        d_copies.append(copy)

    row_tile = min(256, depth)
    steps = []
    for b in range(blocks):
        cols = slice(b * block, (b + 1) * block)
        d_copies[b].wait_recv()

        def grad(k, _):
            at = pl.ds(pl.multiple_of(k * row_tile, row_tile), row_tile)
            total = jnp.dot(acts_t[at], dp[b], preferred_element_type=jnp.float32)
            stepped = nm[at, cols] - learning_rate * total
            nm[at, cols] = stepped
            s_send[b, at] = stepped.astype(jnp.bfloat16)
            return 0

        lax.fori_loop(0, depth // row_tile, grad, 0)
        copy = remote(s_send.at[b], s_recv.at[b], rep_s.at[b], rep_r.at[b], to_rep)
        copy.start()
        steps.append(copy)

    pw_copy.wait()
    out_pw[...] = 0.5 * (pw_send[...] + pw_recv[...])

    outs, sent = [], []
    for b in range(blocks):
        cols = slice(b * block, (b + 1) * block)
        steps[b].wait_recv()

        def mix(k, _):
            at = pl.ds(pl.multiple_of(k * 64, 64), 64)
            nm[at, cols] = 0.5 * (nm[at, cols] + s_recv[b, at].astype(jnp.float32))
            return 0

        lax.fori_loop(0, depth // 64, mix, 0)
        to = pl.ds(pl.multiple_of(core * half + b * block, block), block)
        copy = remote(nm.at[its_rows, cols], out.at[:, to], out_s.at[b], out_r.at[b], to_core)
        copy.start()
        sent.append(copy)
        copy = pltpu.make_async_copy(nm.at[my_rows, cols], out.at[:, to], out_loc.at[b])
        copy.start()
        outs.append(copy)

    for copy in outs:
        copy.wait()
    for copy in sent:
        copy.wait()
    for copy in (*y_attn, *to_other_core, *relays, *p_copies.values(), *stats.values(), *d_copies, *steps):
        copy.wait_send()


def fused(bit, attn, resid, cot, gain, numer, pweight):
    tokens, features = attn.shape
    rows = numer.shape[0]
    half, depth = features // 2, 2 * rows
    chunk = 128
    block = 256 if half % 256 == 0 and half > 256 else 128
    chunks, blocks = tokens // chunk, half // block
    bf16, f32 = jnp.bfloat16, jnp.float32
    sem = pltpu.SemaphoreType.DMA
    scratch = [
        pltpu.VMEM((4 * tokens, depth), bf16),
        pltpu.VMEM((depth, 4 * tokens), bf16),
        pltpu.VMEM((2 * tokens, half), bf16),
        pltpu.VMEM((2 * tokens, half), bf16),
        pltpu.VMEM((1, half), f32),
        pltpu.VMEM((depth, half), f32),
        pltpu.VMEM((depth, half), bf16),
        pltpu.VMEM((2 * tokens, half), f32),
        pltpu.VMEM((2 * tokens, half), bf16),
        pltpu.VMEM((2 * tokens, half), bf16),
        pltpu.VMEM((2 * chunks, 2, chunk, 128), f32),
        pltpu.VMEM((2 * chunks, 2, chunk, 128), f32),
        pltpu.VMEM((2 * tokens, 128), f32),
        pltpu.VMEM((2 * tokens, 128), f32),
        pltpu.VMEM((blocks, 4 * tokens, block), bf16),
        pltpu.VMEM((blocks, depth, block), bf16),
        pltpu.VMEM((blocks, depth, block), bf16),
        pltpu.VMEM((8, 128), f32),
        pltpu.VMEM((8, 128), f32),
        sem((5,)), sem((blocks,)), sem((4,)), sem((4,)),
        sem((chunks,)), sem((chunks,)), sem((2 * chunks,)), sem((2 * chunks,)),
        sem((blocks,)), sem((blocks,)), sem((chunks,)), sem((chunks,)),
        sem((2 * chunks,)), sem((2 * chunks,)), sem((blocks,)), sem((blocks,)),
        sem((blocks,)), sem((blocks,)), sem(()), sem(()),
    ]
    anywhere = pl.BlockSpec(memory_space=pl.ANY)
    return pl.pallas_call(
        functools.partial(fused_kernel, bit, chunk, block),
        out_shape=(
            jax.ShapeDtypeStruct((rows, features), f32),
            jax.ShapeDtypeStruct((8, 128), f32),
        ),
        in_specs=[anywhere] * 5 + [pl.BlockSpec(memory_space=pltpu.SMEM)],
        out_specs=(anywhere, pl.BlockSpec(memory_space=pltpu.VMEM)),
        scratch_shapes=scratch,
        cost_estimate=pl.CostEstimate(
            flops=4 * 4 * tokens * depth * half * 2,
            bytes_accessed=rows * features * 8 + 3 * tokens * features * 2,
            transcendentals=0,
        ),
        compiler_params=pltpu.CompilerParams(
            collective_id=bit, has_side_effects=True, vmem_limit_bytes=56 * 2**20
        ),
        name="push_step_%d" % bit,
    )(attn, resid, cot, gain, numer, pweight)


def on_four(attn, resid, cotangent, gain, numer, pweight, round_bit):
    levels = lax.axis_size("rep").bit_length() - 1
    numer_out, weight_out = lax.switch(
        round_bit[0],
        [functools.partial(fused, level) for level in range(levels)],
        attn[0], resid[0], cotangent[0], gain[None], numer[0], pweight,
    )
    return (numer_out[None], weight_out[0, :1])


def solution(mesh):
    in_specs = (
        P("rep", "shard", None),
        P("rep", "shard", None),
        P("rep", "shard", None),
        P(),
        P("rep", "shard", None),
        P("rep"),
        P(),
    )
    out_specs = (P("rep", "shard", None), P("rep"))
    body = on_four if mesh.shape["shard"] == 4 else on_device
    return jax.shard_map(
        body, mesh=mesh, in_specs=in_specs, out_specs=out_specs, check_vma=False
    )
```

```python
import functools

import jax
import jax.numpy as jnp
from jax import lax
from jax.experimental import pallas as pl
from jax.experimental.pallas import tpu as pltpu
from jax.sharding import PartitionSpec as P

EPS = 1e-05
learning_rate = 0.5


def shortened(shard):

    def short(part):
        return part.astype(jnp.bfloat16) if part.dtype == jnp.float32 else part

    return jax.tree.map(short, shard)


def from_partner(shard, axis, apart):
    return lax.ppermute(shard, axis, [(i, i ^ 1 << apart) for i in range(lax.axis_size(axis))])


def on_device(attn, resid, cotangent, gain, numer, pweight, round_bit):
    acts = attn[0]
    weight_rows = (numer[0] / pweight[0]).astype(jnp.bfloat16)
    columns = acts
    pre = resid[0].astype(jnp.float32) + jnp.dot(
        columns,
        lax.all_gather(weight_rows, "shard", axis=0, tiled=True),
        preferred_element_type=jnp.float32,
    )
    inv = lax.rsqrt(jnp.mean(pre * pre, axis=1, keepdims=True) + EPS)
    normed = pre * inv
    dnorm = cotangent[0].astype(jnp.float32) * gain
    dpre = (inv * (dnorm - normed * jnp.mean(dnorm * normed, axis=1, keepdims=True))).astype(
        jnp.bfloat16
    )
    columns = acts
    grad = lax.psum_scatter(
        lax.dot_general(
            columns, dpre, (((0,), (0,)), ((), ())), preferred_element_type=jnp.float32
        ).astype(jnp.bfloat16),
        "shard",
        scatter_dimension=0,
        tiled=True,
    ).astype(jnp.float32)
    stepped = numer[0] - learning_rate * grad
    levels = lax.axis_size("rep").bit_length() - 1

    def pushed(bit):

        def send_pair(pair):
            return jax.tree.map(
                lambda part, own: part.astype(own.dtype),
                from_partner(shortened(pair), "rep", bit),
                pair,
            )

        return send_pair

    other_numer, other_weight = lax.switch(
        round_bit[0], [pushed(level) for level in range(levels)], (stepped, pweight)
    )
    new_numer = (0.5 * (stepped + other_numer))[None]
    new_pweight = 0.5 * (pweight + other_weight)
    return (new_numer, new_pweight)


def fused_kernel(
    bit, chunk, block,
    attn, resid, cot, gain, numer, pw, out, out_pw,
    acts, acts_t, res, ct, gn1, gn, nm, nm_its, wt, wt_its, pre, p_send, p_recv, st_send, st_recv,
    inv, inv_m, dp, s_send, s_recv, pw_send, pw_recv,
    loc, out_loc, core_s, core_r, relay_s, relay_r, stat_s, stat_r, out_s, out_r,
    ya_s, ya_r, yp_s, yp_r, yd_s, yd_r, rep_s, rep_r, pws_s, pws_r,
):
    tokens, features = attn.shape
    rows = numer.shape[0]
    half = features // 2
    depth = 2 * rows
    chunks = tokens // chunk
    blocks = half // block
    shard = lax.axis_index("shard")
    rep = lax.axis_index("rep")
    core, chip = shard % 2, shard // 2
    apart = 1 << bit
    to_core = {"shard": chip * 2 + 1 - core}
    to_chip = {"shard": (1 - chip) * 2 + core}
    to_rep = {"rep": rep + apart - 2 * apart * ((rep // apart) % 2)}

    def remote(src, dst, send, recv, device):
        return pltpu.make_async_remote_copy(
            src_ref=src, dst_ref=dst, send_sem=send, recv_sem=recv,
            device_id=device, device_id_type=pl.DeviceIdType.MESH,
        )

    my_half = pl.ds(pl.multiple_of(core * half, half), half)
    its_half = pl.ds(pl.multiple_of((1 - core) * half, half), half)
    my_rows = pl.ds(pl.multiple_of(core * rows, rows), rows)
    its_rows = pl.ds(pl.multiple_of((1 - core) * rows, rows), rows)
    my_depth = pl.ds(pl.multiple_of(chip * depth, depth), depth)
    its_depth = pl.ds(pl.multiple_of((1 - chip) * depth, depth), depth)

    local = [
        pltpu.make_async_copy(numer.at[:, its_half], nm_its, loc.at[5]),
        pltpu.make_async_copy(numer.at[:, my_half], nm.at[my_rows], loc.at[0]),
        pltpu.make_async_copy(attn.at[:, my_depth], acts.at[0:tokens], loc.at[1]),
        pltpu.make_async_copy(resid.at[:, my_half], res.at[0:tokens], loc.at[2]),
        pltpu.make_async_copy(cot.at[:, my_half], ct.at[0:tokens], loc.at[3]),
        pltpu.make_async_copy(gain.at[my_half], gn1, loc.at[4]),
    ]
    for copy in local:
        copy.start()

    barrier = pltpu.get_barrier_semaphore()
    for device in (to_core, to_chip, to_rep):
        pl.semaphore_signal(barrier, inc=1, device_id=device, device_id_type=pl.DeviceIdType.MESH)
    pl.semaphore_wait(barrier, 3)

    def part(slot, i):
        return pl.ds(slot * tokens + i * chunk, chunk)

    y_attn = [
        remote(attn.at[pl.ds(i * chunk, chunk), its_depth], acts.at[part(2, i)],
               ya_s.at[i], ya_r.at[i], to_chip)
        for i in range(chunks)
    ]
    for copy in y_attn:
        copy.start()
    to_other_core = [
        remote(wt_its, wt.at[my_rows], core_s.at[4], core_r.at[4], to_core),
        remote(nm_its, nm.at[my_rows], core_s.at[0], core_r.at[0], to_core),
        remote(attn.at[:, my_depth], acts.at[tokens:2 * tokens], core_s.at[1], core_r.at[1], to_core),
        remote(resid.at[:, its_half], res.at[tokens:2 * tokens], core_s.at[2], core_r.at[2], to_core),
        remote(cot.at[:, its_half], ct.at[tokens:2 * tokens], core_s.at[3], core_r.at[3], to_core),
    ]
    weight = pw[0]
    pw_send[...] = jnp.full(pw_send.shape, weight, jnp.float32)
    pw_copy = remote(pw_send, pw_recv, pws_s, pws_r, to_rep)
    pw_copy.start()

    step = 32

    over = (1.0 / pw_send[...])[0:1, 0:1]

    def divide(i, _):
        at = pl.ds(pl.multiple_of(i * step, step), step)
        wt_its[at] = (nm_its[at] * over).astype(jnp.bfloat16)
        return 0

    def divide_mine(i, _):
        at = pl.ds(pl.multiple_of(core * rows + i * step, step), step)
        wt[at] = (nm[at] * over).astype(jnp.bfloat16)
        return 0

    local[0].wait()
    lax.fori_loop(0, rows // step, divide, 0)
    to_other_core[0].start()
    local[1].wait()
    lax.fori_loop(0, rows // step, divide_mine, 0)

    tile = min(256, half)

    def times_weights(at, store):
        def body(j, _):
            cols = pl.ds(pl.multiple_of(j * tile, tile), tile)
            store(cols, jnp.dot(acts[at], wt[:, cols], preferred_element_type=jnp.float32))
            return 0
        lax.fori_loop(0, half // tile, body, 0)

    relays, p_copies = [], {}

    def partial(slot, i):
        at = part(slot, i)

        def store(cols, value):
            p_send[at, cols] = value.astype(jnp.bfloat16)

        times_weights(part(slot + 2, i), store)
        n = 2 * i + slot
        copy = remote(p_send.at[at], p_recv.at[at], yp_s.at[n], yp_r.at[n], to_chip)
        copy.start()
        p_copies[n] = copy

    for i in range(chunks):
        y_attn[i].wait_recv()
        relay = remote(acts.at[part(2, i)], acts.at[part(3, i)], relay_s.at[i], relay_r.at[i], to_core)
        relay.start()
        relays.append(relay)
        if i == 0:
            to_other_core[0].wait_recv()
        partial(0, i)
        relay.wait_recv()
        partial(1, i)

    for copy in (*to_other_core[2:], to_other_core[1]):
        copy.start()
    for copy in local[2:]:
        copy.wait()
    for copy in to_other_core[1:]:
        copy.wait_recv()
    gn[...] = gn1[...].reshape(gn.shape)

    def own(i, _):
        at = pl.ds(pl.multiple_of(i * chunk, chunk), chunk)

        def store(cols, value):
            pre[at, cols] = res[at, cols].astype(jnp.float32) + value

        times_weights(at, store)
        return 0

    lax.fori_loop(0, 2 * chunks, own, 0)

    def turn(i, _):
        at = pl.ds(pl.multiple_of(i * 128, 128), 128)
        acts_t[:, at] = acts[at].T
        return 0

    lax.fori_loop(0, 4 * tokens // 128, turn, 0)

    stats = {}
    for i in range(chunks):
        for slot in range(2):
            n = 2 * i + slot
            p_copies[n].wait_recv()

            def add(k, _):
                at = pl.ds(pl.multiple_of(slot * tokens + i * chunk + k * step, step), step)
                value = pre[at] + p_recv[at].astype(jnp.float32)
                pre[at] = value
                dnorm = ct[at].astype(jnp.float32) * gn[...]
                to = pl.ds(pl.multiple_of(k * step, step), step)
                st_send[n, 0, to] = jnp.broadcast_to(
                    jnp.sum(value * value, axis=1, keepdims=True), (step, 128))
                st_send[n, 1, to] = jnp.broadcast_to(
                    jnp.sum(value * dnorm, axis=1, keepdims=True), (step, 128))
                return 0

            lax.fori_loop(0, chunk // step, add, 0)
            m = 2 * i + 1 - slot
            copy = remote(st_send.at[n], st_recv.at[m], stat_s.at[n], stat_r.at[m], to_core)
            copy.start()
            stats[n] = copy

    for i in range(chunks):
        for slot in range(2):
            n = 2 * i + slot
            m = 2 * i + 1 - slot
            stats[m].wait_recv()
            at = part(slot, i)
            scale = lax.rsqrt((st_send[n, 0] + st_recv[n, 0]) * (1.0 / features) + EPS)
            inv[at] = scale
            inv_m[at] = scale * scale * ((st_send[n, 1] + st_recv[n, 1]) * (1.0 / features))

    d_copies = []
    for b in range(blocks):
        cols = slice(b * block, (b + 1) * block)

        def back(k, _):
            at = pl.ds(pl.multiple_of(k * step, step), step)
            dnorm = ct[at, cols].astype(jnp.float32) * gn[:, cols]
            value = inv[at] * (dnorm - pre[at, cols] * inv_m[at])
            dp[b, at] = value.astype(jnp.bfloat16)
            return 0

        lax.fori_loop(0, 2 * tokens // step, back, 0)
        copy = remote(dp.at[b, 0:2 * tokens], dp.at[b, 2 * tokens:4 * tokens],
                      yd_s.at[b], yd_r.at[b], to_chip)
        copy.start()
        d_copies.append(copy)

    row_tile = min(256, depth)
    steps = []
    for b in range(blocks):
        cols = slice(b * block, (b + 1) * block)
        d_copies[b].wait_recv()

        def grad(k, _):
            at = pl.ds(pl.multiple_of(k * row_tile, row_tile), row_tile)
            total = jnp.dot(acts_t[at], dp[b], preferred_element_type=jnp.float32)
            stepped = nm[at, cols] - learning_rate * total
            nm[at, cols] = stepped
            s_send[b, at] = stepped.astype(jnp.bfloat16)
            return 0

        lax.fori_loop(0, depth // row_tile, grad, 0)
        copy = remote(s_send.at[b], s_recv.at[b], rep_s.at[b], rep_r.at[b], to_rep)
        copy.start()
        steps.append(copy)

    pw_copy.wait()
    out_pw[...] = 0.5 * (pw_send[...] + pw_recv[...])

    outs, sent = [], []
    for b in range(blocks):
        cols = slice(b * block, (b + 1) * block)
        steps[b].wait_recv()

        def mix(k, _):
            at = pl.ds(pl.multiple_of(k * 64, 64), 64)
            nm[at, cols] = 0.5 * (nm[at, cols] + s_recv[b, at].astype(jnp.float32))
            return 0

        lax.fori_loop(0, depth // 64, mix, 0)
        to = pl.ds(pl.multiple_of(core * half + b * block, block), block)
        copy = remote(nm.at[its_rows, cols], out.at[:, to], out_s.at[b], out_r.at[b], to_core)
        copy.start()
        sent.append(copy)
        copy = pltpu.make_async_copy(nm.at[my_rows, cols], out.at[:, to], out_loc.at[b])
        copy.start()
        outs.append(copy)

    for copy in outs:
        copy.wait()
    for copy in sent:
        copy.wait()
    for copy in (*y_attn, *to_other_core, *relays, *p_copies.values(), *stats.values(), *d_copies, *steps):
        copy.wait_send()


def fused(bit, attn, resid, cot, gain, numer, pweight):
    tokens, features = attn.shape
    rows = numer.shape[0]
    half, depth = features // 2, 2 * rows
    chunk = 128
    block = 128
    chunks, blocks = tokens // chunk, half // block
    bf16, f32 = jnp.bfloat16, jnp.float32
    sem = pltpu.SemaphoreType.DMA
    scratch = [
        pltpu.VMEM((4 * tokens, depth), bf16),
        pltpu.VMEM((depth, 4 * tokens), bf16),
        pltpu.VMEM((2 * tokens, half), bf16),
        pltpu.VMEM((2 * tokens, half), bf16),
        pltpu.VMEM((half,), f32),
        pltpu.VMEM((1, half), f32),
        pltpu.VMEM((depth, half), f32),
        pltpu.VMEM((rows, half), f32),
        pltpu.VMEM((depth, half), bf16),
        pltpu.VMEM((rows, half), bf16),
        pltpu.VMEM((2 * tokens, half), f32),
        pltpu.VMEM((2 * tokens, half), bf16),
        pltpu.VMEM((2 * tokens, half), bf16),
        pltpu.VMEM((2 * chunks, 2, chunk, 128), f32),
        pltpu.VMEM((2 * chunks, 2, chunk, 128), f32),
        pltpu.VMEM((2 * tokens, 128), f32),
        pltpu.VMEM((2 * tokens, 128), f32),
        pltpu.VMEM((blocks, 4 * tokens, block), bf16),
        pltpu.VMEM((blocks, depth, block), bf16),
        pltpu.VMEM((blocks, depth, block), bf16),
        pltpu.VMEM((8, 128), f32),
        pltpu.VMEM((8, 128), f32),
        sem((6,)), sem((blocks,)), sem((5,)), sem((5,)),
        sem((chunks,)), sem((chunks,)), sem((2 * chunks,)), sem((2 * chunks,)),
        sem((blocks,)), sem((blocks,)), sem((chunks,)), sem((chunks,)),
        sem((2 * chunks,)), sem((2 * chunks,)), sem((blocks,)), sem((blocks,)),
        sem((blocks,)), sem((blocks,)), sem(()), sem(()),
    ]
    anywhere = pl.BlockSpec(memory_space=pl.ANY)
    return pl.pallas_call(
        functools.partial(fused_kernel, bit, chunk, block),
        out_shape=(
            jax.ShapeDtypeStruct((rows, features), f32),
            jax.ShapeDtypeStruct((8, 128), f32),
        ),
        in_specs=[anywhere] * 5 + [pl.BlockSpec(memory_space=pltpu.SMEM)],
        out_specs=(anywhere, pl.BlockSpec(memory_space=pltpu.VMEM)),
        scratch_shapes=scratch,
        cost_estimate=pl.CostEstimate(
            flops=4 * 4 * tokens * depth * half * 2,
            bytes_accessed=rows * features * 8 + 3 * tokens * features * 2,
            transcendentals=0,
        ),
        compiler_params=pltpu.CompilerParams(
            collective_id=bit, has_side_effects=True, vmem_limit_bytes=56 * 2**20
        ),
        name="push_step_%d" % bit,
    )(attn, resid, cot, gain, numer, pweight)


def on_four(attn, resid, cotangent, gain, numer, pweight, round_bit):
    levels = lax.axis_size("rep").bit_length() - 1
    numer_out, weight_out = lax.switch(
        round_bit[0],
        [functools.partial(fused, level) for level in range(levels)],
        attn[0], resid[0], cotangent[0], gain, numer[0], pweight,
    )
    return (numer_out[None], weight_out[0, :1])


def solution(mesh):
    in_specs = (
        P("rep", "shard", None),
        P("rep", "shard", None),
        P("rep", "shard", None),
        P(),
        P("rep", "shard", None),
        P("rep"),
        P(),
    )
    out_specs = (P("rep", "shard", None), P("rep"))
    body = on_four if mesh.shape["shard"] == 4 else on_device
    return jax.shard_map(
        body, mesh=mesh, in_specs=in_specs, out_specs=out_specs, check_vma=False
    )
```

```python
import functools

import jax
import jax.numpy as jnp
from jax import lax
from jax.experimental import pallas as pl
from jax.experimental.pallas import tpu as pltpu
from jax.sharding import PartitionSpec as P

EPS = 1e-05
learning_rate = 0.5


def shortened(shard):

    def short(part):
        return part.astype(jnp.bfloat16) if part.dtype == jnp.float32 else part

    return jax.tree.map(short, shard)


def from_partner(shard, axis, apart):
    return lax.ppermute(shard, axis, [(i, i ^ 1 << apart) for i in range(lax.axis_size(axis))])


def on_device(attn, resid, cotangent, gain, numer, pweight, round_bit):
    acts = attn[0]
    weight_rows = (numer[0] / pweight[0]).astype(jnp.bfloat16)
    columns = acts
    pre = resid[0].astype(jnp.float32) + jnp.dot(
        columns,
        lax.all_gather(weight_rows, "shard", axis=0, tiled=True),
        preferred_element_type=jnp.float32,
    )
    inv = lax.rsqrt(jnp.mean(pre * pre, axis=1, keepdims=True) + EPS)
    normed = pre * inv
    dnorm = cotangent[0].astype(jnp.float32) * gain
    dpre = (inv * (dnorm - normed * jnp.mean(dnorm * normed, axis=1, keepdims=True))).astype(
        jnp.bfloat16
    )
    columns = acts
    grad = lax.psum_scatter(
        lax.dot_general(
            columns, dpre, (((0,), (0,)), ((), ())), preferred_element_type=jnp.float32
        ).astype(jnp.bfloat16),
        "shard",
        scatter_dimension=0,
        tiled=True,
    ).astype(jnp.float32)
    stepped = numer[0] - learning_rate * grad
    levels = lax.axis_size("rep").bit_length() - 1

    def pushed(bit):

        def send_pair(pair):
            return jax.tree.map(
                lambda part, own: part.astype(own.dtype),
                from_partner(shortened(pair), "rep", bit),
                pair,
            )

        return send_pair

    other_numer, other_weight = lax.switch(
        round_bit[0], [pushed(level) for level in range(levels)], (stepped, pweight)
    )
    new_numer = (0.5 * (stepped + other_numer))[None]
    new_pweight = 0.5 * (pweight + other_weight)
    return (new_numer, new_pweight)


def fused_kernel(
    bit, chunk, block, early,
    attn, resid, cot, gain, numer, pw, out, out_pw,
    acts, acts_t, res, ct, gn1, gn, nm, nm_its, wt, wt_its, pre, p_send, p_recv, st_send, st_recv,
    inv, inv_m, dp, s_send, s_recv, pw_send, pw_recv,
    loc, out_loc, core_s, core_r, relay_s, relay_r, stat_s, stat_r, out_s, out_r,
    ya_s, ya_r, yp_s, yp_r, yd_s, yd_r, rep_s, rep_r, pws_s, pws_r,
    *more,
):
    tokens, features = attn.shape
    rows = numer.shape[0]
    half = features // 2
    depth = 2 * rows
    if early:
        (acts_p, acts_pt, dpp, n_send, n_recv,
         xa_s, xa_r, xr_s, xr_r, xn_s, xn_r, xd_s, xd_r, yy_s, yy_r) = more
    chunks = tokens // chunk
    blocks = half // block
    shard = lax.axis_index("shard")
    rep = lax.axis_index("rep")
    core, chip = shard % 2, shard // 2
    apart = 1 << bit
    to_core = {"shard": chip * 2 + 1 - core}
    to_chip = {"shard": (1 - chip) * 2 + core}
    to_rep = {"rep": rep + apart - 2 * apart * ((rep // apart) % 2)}

    def remote(src, dst, send, recv, device):
        return pltpu.make_async_remote_copy(
            src_ref=src, dst_ref=dst, send_sem=send, recv_sem=recv,
            device_id=device, device_id_type=pl.DeviceIdType.MESH,
        )

    my_half = pl.ds(pl.multiple_of(core * half, half), half)
    its_half = pl.ds(pl.multiple_of((1 - core) * half, half), half)
    my_rows = pl.ds(pl.multiple_of(core * rows, rows), rows)
    its_rows = pl.ds(pl.multiple_of((1 - core) * rows, rows), rows)
    my_depth = pl.ds(pl.multiple_of(chip * depth, depth), depth)
    its_depth = pl.ds(pl.multiple_of((1 - chip) * depth, depth), depth)

    local = [
        pltpu.make_async_copy(numer.at[:, its_half], nm_its, loc.at[5]),
        pltpu.make_async_copy(numer.at[:, my_half], nm.at[my_rows], loc.at[0]),
        pltpu.make_async_copy(attn.at[:, my_depth], acts.at[0:tokens], loc.at[1]),
        pltpu.make_async_copy(resid.at[:, my_half], res.at[0:tokens], loc.at[2]),
        pltpu.make_async_copy(cot.at[:, my_half], ct.at[0:tokens], loc.at[3]),
        pltpu.make_async_copy(gain.at[my_half], gn1, loc.at[4]),
    ]
    for copy in local:
        copy.start()

    barrier = pltpu.get_barrier_semaphore()
    for device in (to_core, to_chip, to_rep):
        pl.semaphore_signal(barrier, inc=1, device_id=device, device_id_type=pl.DeviceIdType.MESH)
    pl.semaphore_wait(barrier, 3)

    def part(slot, i):
        return pl.ds(slot * tokens + i * chunk, chunk)

    y_attn = [
        remote(attn.at[pl.ds(i * chunk, chunk), its_depth], acts.at[part(2, i)],
               ya_s.at[i], ya_r.at[i], to_chip)
        for i in range(chunks)
    ]
    for copy in y_attn:
        copy.start()
    to_other_core = [
        remote(wt_its, wt.at[my_rows], core_s.at[4], core_r.at[4], to_core),
        remote(nm_its, nm.at[my_rows], core_s.at[0], core_r.at[0], to_core),
        remote(attn.at[:, my_depth], acts.at[tokens:2 * tokens], core_s.at[1], core_r.at[1], to_core),
        remote(resid.at[:, its_half], res.at[tokens:2 * tokens], core_s.at[2], core_r.at[2], to_core),
        remote(cot.at[:, its_half], ct.at[tokens:2 * tokens], core_s.at[3], core_r.at[3], to_core),
    ]
    weight = pw[0]
    pw_send[...] = jnp.full(pw_send.shape, weight, jnp.float32)
    pw_copy = remote(pw_send, pw_recv, pws_s, pws_r, to_rep)
    pw_copy.start()

    step = 32

    over = (1.0 / pw_send[...])[0:1, 0:1]

    def divide(i, _):
        at = pl.ds(pl.multiple_of(i * step, step), step)
        wt_its[at] = (nm_its[at] * over).astype(jnp.bfloat16)
        return 0

    def divide_mine(i, _):
        at = pl.ds(pl.multiple_of(core * rows + i * step, step), step)
        wt[at] = (nm[at] * over).astype(jnp.bfloat16)
        return 0

    x_acts, x_relays, x_numer, x_dp, y_dp = [], [], [], [], []

    def send_acts(k):
        at = pl.ds(2 * k * tokens, tokens)
        copy = remote(acts.at[at], acts_p.at[at], xa_s.at[k], xa_r.at[k], to_rep)
        copy.start()
        x_acts.append(copy)

    if early:
        local[2].wait()
        send_acts(0)

    local[0].wait()
    lax.fori_loop(0, rows // step, divide, 0)
    to_other_core[0].start()
    local[1].wait()
    lax.fori_loop(0, rows // step, divide_mine, 0)

    tile = min(256, half)

    def times_weights(at, store):
        def body(j, _):
            cols = pl.ds(pl.multiple_of(j * tile, tile), tile)
            store(cols, jnp.dot(acts[at], wt[:, cols], preferred_element_type=jnp.float32))
            return 0
        lax.fori_loop(0, half // tile, body, 0)

    relays, p_copies = [], {}

    def partial(slot, i):
        at = part(slot, i)

        def store(cols, value):
            p_send[at, cols] = value.astype(jnp.bfloat16)

        times_weights(part(slot + 2, i), store)
        n = 2 * i + slot
        copy = remote(p_send.at[at], p_recv.at[at], yp_s.at[n], yp_r.at[n], to_chip)
        copy.start()
        p_copies[n] = copy

    for i in range(chunks):
        y_attn[i].wait_recv()
        relay = remote(acts.at[part(2, i)], acts.at[part(3, i)], relay_s.at[i], relay_r.at[i], to_core)
        relay.start()
        relays.append(relay)
        if i == 0:
            to_other_core[0].wait_recv()
        partial(0, i)
        relay.wait_recv()
        partial(1, i)

    for copy in (*to_other_core[2:], to_other_core[1]):
        copy.start()
    if early:
        send_acts(1)
    for copy in local[3 if early else 2:]:
        copy.wait()
    for copy in to_other_core[1:]:
        copy.wait_recv()
    gn[...] = gn1[...].reshape(gn.shape)
    for b in range(early):
        cols = slice(b * block, (b + 1) * block)

        def shorten(k, _):
            at = pl.ds(pl.multiple_of(k * 64, 64), 64)
            n_send[b, at] = nm[at, cols].astype(jnp.bfloat16)
            return 0

        lax.fori_loop(0, depth // 64, shorten, 0)
        copy = remote(n_send.at[b], n_recv.at[b], xn_s.at[b], xn_r.at[b], to_rep)
        copy.start()
        x_numer.append(copy)

    def own(i, _):
        at = pl.ds(pl.multiple_of(i * chunk, chunk), chunk)

        def store(cols, value):
            pre[at, cols] = res[at, cols].astype(jnp.float32) + value

        times_weights(at, store)
        return 0

    lax.fori_loop(0, 2 * chunks, own, 0)

    def turn(i, _):
        at = pl.ds(pl.multiple_of(i * 128, 128), 128)
        acts_t[:, at] = acts[at].T
        return 0

    lax.fori_loop(0, 4 * tokens // 128, turn, 0)

    if early:
        for k in range(2):
            x_acts[k].wait_recv()
            copy = remote(acts_p.at[pl.ds(2 * k * tokens, tokens)],
                          acts_p.at[pl.ds((2 * k + 1) * tokens, tokens)],
                          xr_s.at[k], xr_r.at[k], to_core)
            copy.start()
            x_relays.append(copy)
        for copy in x_relays:
            copy.wait_recv()

        def turn_p(i, _):
            at = pl.ds(pl.multiple_of(i * 128, 128), 128)
            acts_pt[:, at] = acts_p[at].T
            return 0

        lax.fori_loop(0, 4 * tokens // 128, turn_p, 0)

    stats = {}
    for i in range(chunks):
        for slot in range(2):
            n = 2 * i + slot
            p_copies[n].wait_recv()

            def add(k, _):
                at = pl.ds(pl.multiple_of(slot * tokens + i * chunk + k * step, step), step)
                value = pre[at] + p_recv[at].astype(jnp.float32)
                pre[at] = value
                dnorm = ct[at].astype(jnp.float32) * gn[...]
                to = pl.ds(pl.multiple_of(k * step, step), step)
                st_send[n, 0, to] = jnp.broadcast_to(
                    jnp.sum(value * value, axis=1, keepdims=True), (step, 128))
                st_send[n, 1, to] = jnp.broadcast_to(
                    jnp.sum(value * dnorm, axis=1, keepdims=True), (step, 128))
                return 0

            lax.fori_loop(0, chunk // step, add, 0)
            m = 2 * i + 1 - slot
            copy = remote(st_send.at[n], st_recv.at[m], stat_s.at[n], stat_r.at[m], to_core)
            copy.start()
            stats[n] = copy

    for i in range(chunks):
        for slot in range(2):
            n = 2 * i + slot
            m = 2 * i + 1 - slot
            stats[m].wait_recv()
            at = part(slot, i)
            scale = lax.rsqrt((st_send[n, 0] + st_recv[n, 0]) * (1.0 / features) + EPS)
            inv[at] = scale
            inv_m[at] = scale * scale * ((st_send[n, 1] + st_recv[n, 1]) * (1.0 / features))

    d_copies = []
    for b in range(blocks):
        cols = slice(b * block, (b + 1) * block)

        def back(k, _):
            at = pl.ds(pl.multiple_of(k * step, step), step)
            dnorm = ct[at, cols].astype(jnp.float32) * gn[:, cols]
            value = inv[at] * (dnorm - pre[at, cols] * inv_m[at])
            dp[b, at] = value.astype(jnp.bfloat16)
            return 0

        lax.fori_loop(0, 2 * tokens // step, back, 0)
        copy = remote(dp.at[b, 0:2 * tokens], dp.at[b, 2 * tokens:4 * tokens],
                      yd_s.at[b], yd_r.at[b], to_chip)
        d_copies.append(copy)
        if b >= early:
            copy.start()
        else:
            copy = remote(dp.at[b, 0:2 * tokens], dpp.at[b, 0:2 * tokens],
                          xd_s.at[b], xd_r.at[b], to_rep)
            copy.start()
            x_dp.append(copy)
    for copy in d_copies[:early]:
        copy.start()

    def pass_on():
        b = len(y_dp)
        x_dp[b].wait_recv()
        copy = remote(dpp.at[b, 0:2 * tokens], dpp.at[b, 2 * tokens:4 * tokens],
                      yy_s.at[b], yy_r.at[b], to_chip)
        copy.start()
        y_dp.append(copy)

    row_tile = min(256, depth)
    steps = {}
    for b in range(early, blocks):
        cols = slice(b * block, (b + 1) * block)
        d_copies[b].wait_recv()

        def grad(k, _):
            at = pl.ds(pl.multiple_of(k * row_tile, row_tile), row_tile)
            total = jnp.dot(acts_t[at], dp[b], preferred_element_type=jnp.float32)
            stepped = nm[at, cols] - learning_rate * total
            nm[at, cols] = stepped
            s_send[b, at] = stepped.astype(jnp.bfloat16)
            return 0

        lax.fori_loop(0, depth // row_tile, grad, 0)
        copy = remote(s_send.at[b], s_recv.at[b], rep_s.at[b], rep_r.at[b], to_rep)
        copy.start()
        steps[b] = copy
        if b > early and len(y_dp) < early:
            pass_on()
    while len(y_dp) < early:
        pass_on()

    pw_copy.wait()
    out_pw[...] = 0.5 * (pw_send[...] + pw_recv[...])

    outs, sent = [], []
    last = max(early, blocks - 2)
    for b in (*range(early, last), *range(early), *range(last, blocks)):
        cols = slice(b * block, (b + 1) * block)

        def mix(k, _):
            at = pl.ds(pl.multiple_of(k * 64, 64), 64)
            nm[at, cols] = 0.5 * (nm[at, cols] + s_recv[b, at].astype(jnp.float32))
            return 0

        def mix_early(k, _):
            at = pl.ds(pl.multiple_of(k * row_tile, row_tile), row_tile)
            mine = jnp.dot(acts_t[at], dp[b], preferred_element_type=jnp.float32)
            its = jnp.dot(acts_pt[at], dpp[b], preferred_element_type=jnp.float32)
            stepped = nm[at, cols] - learning_rate * mine
            other = n_recv[b, at].astype(jnp.float32) - learning_rate * its
            nm[at, cols] = 0.5 * (stepped + other)
            return 0

        if b < early:
            d_copies[b].wait_recv()
            y_dp[b].wait_recv()
            x_numer[b].wait_recv()
            lax.fori_loop(0, depth // row_tile, mix_early, 0)
        else:
            steps[b].wait_recv()
            lax.fori_loop(0, depth // 64, mix, 0)
        to = pl.ds(pl.multiple_of(core * half + b * block, block), block)
        copy = remote(nm.at[its_rows, cols], out.at[:, to], out_s.at[b], out_r.at[b], to_core)
        copy.start()
        sent.append(copy)
        copy = pltpu.make_async_copy(nm.at[my_rows, cols], out.at[:, to], out_loc.at[b])
        copy.start()
        outs.append(copy)

    for copy in outs:
        copy.wait()
    for copy in sent:
        copy.wait()
    for copy in (*y_attn, *to_other_core, *relays, *p_copies.values(), *stats.values(), *d_copies, *steps.values(),
                 *x_acts, *x_relays, *x_numer, *x_dp, *y_dp):
        copy.wait_send()


def fused(bit, attn, resid, cot, gain, numer, pweight):
    tokens, features = attn.shape
    rows = numer.shape[0]
    half, depth = features // 2, 2 * rows
    chunk = 128
    block = 128
    chunks, blocks = tokens // chunk, half // block
    bf16, f32 = jnp.bfloat16, jnp.float32
    sem = pltpu.SemaphoreType.DMA
    scratch = [
        pltpu.VMEM((4 * tokens, depth), bf16),
        pltpu.VMEM((depth, 4 * tokens), bf16),
        pltpu.VMEM((2 * tokens, half), bf16),
        pltpu.VMEM((2 * tokens, half), bf16),
        pltpu.VMEM((half,), f32),
        pltpu.VMEM((1, half), f32),
        pltpu.VMEM((depth, half), f32),
        pltpu.VMEM((rows, half), f32),
        pltpu.VMEM((depth, half), bf16),
        pltpu.VMEM((rows, half), bf16),
        pltpu.VMEM((2 * tokens, half), f32),
        pltpu.VMEM((2 * tokens, half), bf16),
        pltpu.VMEM((2 * tokens, half), bf16),
        pltpu.VMEM((2 * chunks, 2, chunk, 128), f32),
        pltpu.VMEM((2 * chunks, 2, chunk, 128), f32),
        pltpu.VMEM((2 * tokens, 128), f32),
        pltpu.VMEM((2 * tokens, 128), f32),
        pltpu.VMEM((blocks, 4 * tokens, block), bf16),
        pltpu.VMEM((blocks, depth, block), bf16),
        pltpu.VMEM((blocks, depth, block), bf16),
        pltpu.VMEM((8, 128), f32),
        pltpu.VMEM((8, 128), f32),
        sem((6,)), sem((blocks,)), sem((5,)), sem((5,)),
        sem((chunks,)), sem((chunks,)), sem((2 * chunks,)), sem((2 * chunks,)),
        sem((blocks,)), sem((blocks,)), sem((chunks,)), sem((chunks,)),
        sem((2 * chunks,)), sem((2 * chunks,)), sem((blocks,)), sem((blocks,)),
        sem((blocks,)), sem((blocks,)), sem(()), sem(()),
    ]
    early = min(3, blocks - 1) if bit < 2 else 0
    if early:
        scratch += [
            pltpu.VMEM((4 * tokens, depth), bf16),
            pltpu.VMEM((depth, 4 * tokens), bf16),
            pltpu.VMEM((early, 4 * tokens, block), bf16),
            pltpu.VMEM((early, depth, block), bf16),
            pltpu.VMEM((early, depth, block), bf16),
            *[sem((2,))] * 4,
            *[sem((early,))] * 6,
        ]
    anywhere = pl.BlockSpec(memory_space=pl.ANY)
    return pl.pallas_call(
        functools.partial(fused_kernel, bit, chunk, block, early),
        out_shape=(
            jax.ShapeDtypeStruct((rows, features), f32),
            jax.ShapeDtypeStruct((8, 128), f32),
        ),
        in_specs=[anywhere] * 5 + [pl.BlockSpec(memory_space=pltpu.SMEM)],
        out_specs=(anywhere, pl.BlockSpec(memory_space=pltpu.VMEM)),
        scratch_shapes=scratch,
        cost_estimate=pl.CostEstimate(
            flops=4 * 4 * tokens * depth * half * 2,
            bytes_accessed=rows * features * 8 + 3 * tokens * features * 2,
            transcendentals=0,
        ),
        compiler_params=pltpu.CompilerParams(
            collective_id=bit, has_side_effects=True, vmem_limit_bytes=60 * 2**20
        ),
        name="push_step_%d" % bit,
    )(attn, resid, cot, gain, numer, pweight)


def on_four(attn, resid, cotangent, gain, numer, pweight, round_bit):
    levels = lax.axis_size("rep").bit_length() - 1
    numer_out, weight_out = lax.switch(
        round_bit[0],
        [functools.partial(fused, level) for level in range(levels)],
        attn[0], resid[0], cotangent[0], gain, numer[0], pweight,
    )
    return (numer_out[None], weight_out[0, :1])


def solution(mesh):
    in_specs = (
        P("rep", "shard", None),
        P("rep", "shard", None),
        P("rep", "shard", None),
        P(),
        P("rep", "shard", None),
        P("rep"),
        P(),
    )
    out_specs = (P("rep", "shard", None), P("rep"))
    body = on_four if mesh.shape["shard"] == 4 else on_device
    return jax.shard_map(
        body, mesh=mesh, in_specs=in_specs, out_specs=out_specs, check_vma=False
    )
```
